256 devices in a mesh: ctx: 16 (over x_lo, y, core), head: 16 (over z, x_hi).
Axes of the slice: x: 4 (x_hi: 2, x_lo: 2; x = x_hi * 2 + x_lo), y: 4, z: 8, core: 2. Of those that a mesh axis runs over, the one named last changes fastest.
Arguments:
- tokens: bfloat16 [16384, 5376], P('ctx', 'head'), may hold values from -48 to 48
- w_qkv: bfloat16 [5376, 8192], P('ctx', 'head')
Outputs:
- attended: bfloat16 [16384, 4096], P('ctx', 'head')
The draws below stay inside these ranges and needn't reach their ends.
All inputs are finite; a program needn't handle non-finite values.
Results may differ from the reference program's by a relative error of at most 0.011.
Values may be sent and summed in bfloat16 or wider, within the bound.
No kernel may reach another device: no remote copies, remote signals or barrier semaphores. Data moves between devices by JAX's collectives and lax.ppermute only.
A program may use at most 128 MiB of HBM per device.

```python
import math
import jax
import jax.numpy as jnp
from jax import lax

D = 5376
HEAD_DIM = 128
Q_PER_KV = 2
WINDOW = 1024
KV_HEADS = 16
TOKENS = 16384


def draw_tokens(key, part):
    normal_part = jnp.clip(jax.random.normal(jax.random.fold_in(key, 11), (TOKENS, D), jnp.float32), -6.0, 6.0)
    return normal_part.astype(jnp.bfloat16)


def draw_w_qkv(key, part):
    full_shape = (D, KV_HEADS, Q_PER_KV + 2, HEAD_DIM)
    normal_part = jnp.clip(jax.random.normal(jax.random.fold_in(key, 21), full_shape, jnp.float32), -4.0, 4.0)
    return (normal_part / math.sqrt(D)).reshape(D, KV_HEADS * (Q_PER_KV + 2) * HEAD_DIM).astype(jnp.bfloat16)


def setup_inputs(seed: int = 0) -> dict:
    key_list = jax.random.split(jax.random.key(seed), 3)
    return {
        "tokens": draw_tokens(jax.random.fold_in(key_list[2], 71), 0),
        "w_qkv": draw_w_qkv(jax.random.fold_in(key_list[2], 71), 0),
    }


rope_base = 10000.0
query_scale = 168.0 ** -0.5
masked_score = -1.0e30


def rotate(projected, positions):
    head_width = projected.shape[-1]
    half_width = head_width // 2
    inverse = jnp.power(rope_base, -2.0 * jnp.arange(half_width, dtype=jnp.float32) / head_width)
    angles = positions.astype(jnp.float32)[:, None] * inverse[None, :]
    target_shape = (projected.shape[0],) + (1,) * (projected.ndim - 2) + (half_width,)
    cosine = jnp.cos(angles).reshape(target_shape)
    sine_part = jnp.sin(angles).reshape(target_shape)
    leading = projected[..., :half_width]
    second = projected[..., half_width:]
    return jnp.concatenate([leading * cosine - second * sine_part, second * cosine + leading * sine_part], axis=-1)


def attend(queries, key_rows, value_rows, key_anchor):
    row_count = queries.shape[0]
    block_rows = min(512, row_count)
    span = key_rows.shape[0] - row_count
    query_pos = jnp.arange(block_rows, dtype=jnp.int32)[:, None]
    key_pos = jnp.arange(block_rows + span, dtype=jnp.int32)[None, :]

    def one_block(block_index):
        first_row = (block_index * block_rows).astype(jnp.int32)
        query_block = lax.dynamic_slice_in_dim(queries, first_row, block_rows, 0).astype(jnp.float32)
        key_block = lax.dynamic_slice_in_dim(key_rows, first_row, block_rows + span, 0).astype(jnp.float32)
        value_block = lax.dynamic_slice_in_dim(value_rows, first_row, block_rows + span, 0).astype(jnp.float32)
        scores = jnp.einsum("qkgd,ckd->kgqc", query_block, key_block) * query_scale
        allowed = (key_pos > query_pos) & (key_pos <= query_pos + span) & (key_anchor + first_row + key_pos >= 0)
        scores = jnp.where(allowed[None, None], scores, masked_score)
        highest = jnp.max(scores, axis=-1, keepdims=True)
        expanded = jnp.exp(scores - highest)
        probabilities = (expanded / jnp.sum(expanded, axis=-1, keepdims=True)).astype(jnp.bfloat16)
        summed = jnp.einsum("kgqc,ckd->qkgd", probabilities.astype(jnp.float32), value_block)
        return summed.astype(jnp.bfloat16)

    attended = lax.map(one_block, jnp.arange(row_count // block_rows, dtype=jnp.int32))
    return attended.reshape(row_count, -1)


def reference(tokens, w_qkv):
    row_count = tokens.shape[0]
    projected = jnp.dot(tokens, w_qkv, preferred_element_type=jnp.float32)
    projected = projected.reshape(row_count, KV_HEADS, Q_PER_KV + 2, HEAD_DIM)
    positions = jnp.arange(row_count, dtype=jnp.int32)
    queries = rotate(projected[:, :, :Q_PER_KV], positions).astype(jnp.bfloat16)
    key_rows = rotate(projected[:, :, Q_PER_KV], positions).astype(jnp.bfloat16)
    value_rows = projected[:, :, Q_PER_KV + 1].astype(jnp.bfloat16)
    padding = jnp.zeros((WINDOW, KV_HEADS, HEAD_DIM), jnp.bfloat16)
    key_rows = jnp.concatenate([padding, key_rows], axis=0)
    value_rows = jnp.concatenate([padding, value_rows], axis=0)
    return attend(queries, key_rows, value_rows, jnp.int32(-WINDOW))
```

```python
import functools

import jax
import jax.numpy as jnp
from jax import lax
from jax.experimental import pallas as pl
from jax.experimental.pallas import tpu as pltpu
from jax.sharding import Mesh
from jax.sharding import PartitionSpec as P

HEAD = 128
Q_PER_KV = 2
WINDOW = 1024
ROPE_BASE = 10000.0
SCALE = 168.0 ** (-0.5)
LOG2E = 1.4426950408889634
MASKED = -1e30

AXES = ("x_lo", "y", "core", "z", "x_hi")
SIZES = (2, 4, 2, 8, 2)
CTX = ("x_lo", "y", "core")
HEADS = ("z", "x_hi")

CHUNKS = 2
TILE = 256
VMEM_BYTES = 40 * 1024 * 1024


def hop(block, axis, distance):
    n = lax.axis_size(axis)
    return lax.ppermute(block, axis, [(i, (i + distance) % n) for i in range(n)])


def swap(block, axis):
    return lax.ppermute(block, axis, [(0, 1), (1, 0)])


def ring_over_z(chunks):
    got = [[(0, chunk)] for chunk in chunks]
    forward, backward = list(chunks), list(chunks)
    for step in range(1, 5):
        for i in range(len(chunks)):
            if step < 4 or i % 2 == 0:
                forward[i] = hop(forward[i], "z", 1)
                got[i].append((-step, forward[i]))
            if step < 4 or i % 2 == 1:
                backward[i] = hop(backward[i], "z", -1)
                got[i].append((step, backward[i]))
    return got


def gather_weights(w):
    core, x_hi = lax.axis_index("core"), lax.axis_index("x_hi")
    crossed = lax.ppermute(w, ("core", "x_hi"), [(1, 2), (2, 1)])
    mine = jnp.where(core == x_hi, w, crossed)
    pair = jnp.stack([mine, swap(mine, "x_lo")])
    blocks = [pair] + [hop(pair, "y", d) for d in (1, 2, 3)]
    return blocks + [swap(b, "core") for b in blocks]


def product_kernel(distances, has_acc, where_ref, *refs):
    n = len(distances)
    tokens, weights = refs[:n], refs[n : n + 8]
    refs = refs[n + 8 :]
    acc_ref, refs = (refs[0], refs[1:]) if has_acc else (None, refs)
    out_ref, tok, wts, tok_sem, wts_sem = refs
    depth = tokens[0].shape[0]
    case = where_ref[0]
    for j in range(n):
        pltpu.make_async_copy(tokens[j], tok.at[pl.ds(j * depth, depth)], tok_sem.at[j]).start()
    for half in range(2):
        for k in range(4):

            @pl.when(case == half * 4 + k)
            def _(half=half, k=k):
                for j, d in enumerate(distances):
                    source = weights[half * 4 + (k - d) % 4].at[where_ref[1 + d % 8]]
                    pltpu.make_async_copy(
                        source, wts.at[pl.ds(j * depth, depth)], wts_sem.at[j]
                    ).start()

    for j in range(n):
        pltpu.make_async_copy(tokens[j], tok.at[pl.ds(j * depth, depth)], tok_sem.at[j]).wait()
        pltpu.make_async_copy(
            weights[0].at[0], wts.at[pl.ds(j * depth, depth)], wts_sem.at[j]
        ).wait()
    total = lax.dot_general(
        tok[...], wts[...], (((0,), (0,)), ((), ())), preferred_element_type=jnp.float32
    )
    if has_acc:
        total = total + acc_ref[...]
    out_ref[...] = total.astype(out_ref.dtype)


def product(where, shards, weights, acc, dtype):
    distances = tuple(d for d, _ in shards)
    tokens = [t for _, t in shards]
    depth, rows = tokens[0].shape
    columns = weights[0].shape[-1]
    n = len(tokens)
    hbm = pl.BlockSpec(memory_space=pl.ANY)
    vmem = pl.BlockSpec(memory_space=pltpu.VMEM)
    operands = [where, *tokens, *weights]
    specs = [pl.BlockSpec(memory_space=pltpu.SMEM)] + [hbm] * (n + 8)
    if acc is not None:
        operands.append(acc)
        specs.append(vmem)
    return pl.pallas_call(
        functools.partial(product_kernel, distances, acc is not None),
        out_shape=jax.ShapeDtypeStruct((rows, columns), dtype),
        in_specs=specs,
        out_specs=vmem,
        scratch_shapes=[
            pltpu.VMEM((n * depth, rows), jnp.bfloat16),
            pltpu.VMEM((n * depth, columns), jnp.bfloat16),
            pltpu.SemaphoreType.DMA((n,)),
            pltpu.SemaphoreType.DMA((n,)),
        ],
        compiler_params=pltpu.CompilerParams(vmem_limit_bytes=VMEM_BYTES),
        cost_estimate=pl.CostEstimate(
            flops=2 * n * depth * rows * columns,
            bytes_accessed=2 * n * depth * (rows + columns) + 4 * rows * columns,
            transcendentals=0,
        ),
    )(*operands)


def finish_kernel(keep_ref, sent_ref, cos_ref, sin_ref, q_ref, kv_ref):
    cos, sin = cos_ref[...], sin_ref[...]
    for j in range(4):
        columns = pl.ds(j * HEAD, HEAD)
        block = keep_ref[:, columns] + sent_ref[:, columns].astype(jnp.float32)
        if j < 3:
            block = block * cos + pltpu.roll(block, HEAD // 2, 1) * sin
        block = block.astype(jnp.bfloat16)
        if j < 2:
            q_ref[:, columns] = block
        else:
            kv_ref[:, pl.ds((j - 2) * HEAD, HEAD)] = block


def finish(keep, sent, cos, sin):
    rows = keep.shape[0]
    vmem = pl.BlockSpec(memory_space=pltpu.VMEM)
    return pl.pallas_call(
        finish_kernel,
        out_shape=[jax.ShapeDtypeStruct((rows, 2 * HEAD), jnp.bfloat16)] * 2,
        in_specs=[vmem] * 4,
        out_specs=[vmem] * 2,
        compiler_params=pltpu.CompilerParams(vmem_limit_bytes=VMEM_BYTES),
        cost_estimate=pl.CostEstimate(
            flops=rows * 2048, bytes_accessed=rows * 6000, transcendentals=0
        ),
    )(keep, sent, cos, sin)


def attend_kernel(chunks, first_ref, *refs):
    q_refs, own_refs, before_refs = refs[:chunks], refs[chunks : 2 * chunks], refs[2 * chunks : 3 * chunks]
    out_ref = refs[3 * chunks]
    rows = q_refs[0].shape[0]
    per_chunk = rows // TILE
    tiles = chunks * per_chunk
    outside = jnp.where(first_ref[0] == 0, jnp.float32(MASKED), jnp.float32(0))
    row = lax.broadcasted_iota(jnp.int32, (2 * TILE, TILE), 0) % TILE
    column = lax.broadcasted_iota(jnp.int32, (2 * TILE, TILE), 1)
    later = column > row

    def piece(group, tile, start):
        ref = group[tile // per_chunk]
        return ref[pl.ds(tile % per_chunk * TILE, TILE), pl.ds(start, HEAD)]

    for i in range(tiles):
        q = jnp.concatenate([piece(q_refs, i, 0), piece(q_refs, i, HEAD)], axis=0)
        scores = []
        for t in range(tiles + 1):
            source, tile = (before_refs, i + t) if i + t < tiles else (own_refs, i + t - tiles)
            s = lax.dot_general(
                q,
                piece(source, tile, 0),
                (((1,), (1,)), ((), ())),
                preferred_element_type=jnp.float32,
            )
            if i + t < tiles:
                s = s + outside
            if t == 0:
                s = jnp.where(later, s, MASKED)
            if t == tiles:
                s = jnp.where(later, MASKED, s)
            scores.append(s)
        highest = functools.reduce(jnp.maximum, scores)
        highest = jnp.max(highest, axis=-1, keepdims=True)
        shift = highest * (SCALE * LOG2E)
        total, summed = None, None
        for t in range(tiles + 1):
            source, tile = (before_refs, i + t) if i + t < tiles else (own_refs, i + t - tiles)
            p = jnp.exp2(scores[t] * (SCALE * LOG2E) - shift)
            total = p if total is None else total + p
            part = jnp.dot(
                p.astype(jnp.bfloat16),
                piece(source, tile, HEAD),
                preferred_element_type=jnp.float32,
            )
            summed = part if summed is None else summed + part
        total = jnp.sum(total, axis=-1, keepdims=True)
        out = (summed / total).astype(jnp.bfloat16)
        out_ref[pl.ds(i * TILE, TILE), pl.ds(0, HEAD)] = out[:TILE]
        out_ref[pl.ds(i * TILE, TILE), pl.ds(HEAD, HEAD)] = out[TILE:]


def attend(first, queries, own, before):
    chunks = len(queries)
    rows = queries[0].shape[0]
    vmem = pl.BlockSpec(memory_space=pltpu.VMEM)
    return pl.pallas_call(
        functools.partial(attend_kernel, chunks),
        out_shape=jax.ShapeDtypeStruct((chunks * rows, 2 * HEAD), jnp.bfloat16),
        in_specs=[pl.BlockSpec(memory_space=pltpu.SMEM)] + [vmem] * (3 * chunks),
        out_specs=vmem,
        compiler_params=pltpu.CompilerParams(vmem_limit_bytes=VMEM_BYTES),
        cost_estimate=pl.CostEstimate(
            flops=2 * 2 * 2 * chunks * rows * (WINDOW + TILE) * HEAD,
            bytes_accessed=chunks * rows * 2048,
            transcendentals=2 * chunks * rows * (WINDOW + TILE),
        ),
    )(first, *queries, *own, *before)


def rotary_tables(positions):
    half = HEAD // 2
    inverse = jnp.power(ROPE_BASE, -2.0 * jnp.arange(half, dtype=jnp.float32) / HEAD)
    angles = positions.astype(jnp.float32)[:, None] * inverse[None, :]
    cos, sin = jnp.cos(angles), jnp.sin(angles)
    return jnp.concatenate([cos, cos], axis=1), jnp.concatenate([-sin, sin], axis=1)


def on_device(tokens, w_qkv):
    row_count = tokens.shape[0]
    rows = row_count // CHUNKS
    x_lo, y, core, z, x_hi = (lax.axis_index(a) for a in AXES)
    ctx = (x_lo * 4 + y) * 2 + core
    positions = ctx * row_count + jnp.arange(row_count, dtype=jnp.int32)
    cos, sin = rotary_tables(positions)

    away = (z + jnp.arange(8, dtype=jnp.int32)) % 8
    x_rel = (x_lo + away // 4) % 2
    keep_half = jnp.where(core == x_hi, 0, 1)
    y_rel = (y - z) % 4

    def where(half):
        return jnp.concatenate([(half * 4 + y_rel)[None], x_rel]).astype(jnp.int32)

    keep_where, send_where = where(keep_half), where(1 - keep_half)

    shards = ring_over_z([tokens[i * rows : (i + 1) * rows].T for i in range(CHUNKS)])
    weights = gather_weights(w_qkv)

    queries, own, before = [], [], []
    for i in range(CHUNKS):
        early, late = shards[i][:5], shards[i][5:]
        send = product(send_where, early, weights, None, jnp.float32)
        keep = product(keep_where, early, weights, None, jnp.float32)
        send = product(send_where, late, weights, send, jnp.bfloat16)
        sent = swap(send, "x_hi")
        keep = product(keep_where, late, weights, keep, jnp.float32)
        span = slice(i * rows, (i + 1) * rows)
        q, kv = finish(keep, sent, cos[span], sin[span])
        queries.append(q)
        own.append(kv)
        before.append(lax.ppermute(kv, CTX, [(c, c + 1) for c in range(15)]))
    return attend(ctx.astype(jnp.int32)[None], queries, own, before)


def solution(mesh):
    fine = Mesh(mesh.devices.reshape(SIZES), AXES)
    placed = P(CTX, HEADS)
    return jax.shard_map(
        on_device, mesh=fine, in_specs=(placed, placed), out_specs=placed, check_vma=False
    )
```

```python
import functools

import jax
import jax.numpy as jnp
from jax import lax
from jax.experimental import pallas as pl
from jax.experimental.pallas import tpu as pltpu
from jax.sharding import Mesh
from jax.sharding import PartitionSpec as P

HEAD = 128
Q_PER_KV = 2
WINDOW = 1024
ROPE_BASE = 10000.0
SCALE = 168.0 ** (-0.5)
LOG2E = 1.4426950408889634
MASKED = -1e30

AXES = ("x_lo", "y", "core", "z", "x_hi")
SIZES = (2, 4, 2, 8, 2)
CTX = ("x_lo", "y", "core")
HEADS = ("z", "x_hi")

TILE = 256
DISTANCES = (0, -1, 1, -2, 2, -3, 3, 4)
VMEM_BYTES = 12 * 1024 * 1024


def hop(block, axis, distance):
    n = lax.axis_size(axis)
    return lax.ppermute(block, axis, [(i, (i + distance) % n) for i in range(n)])


def swap(block, axis):
    return lax.ppermute(block, axis, [(0, 1), (1, 0)])


def after(value, *others):
    return lax.optimization_barrier((value, *others))[0]


def gather(tokens, w, where, tables):
    core, x_hi = lax.axis_index("core"), lax.axis_index("x_hi")
    tie = lax.optimization_barrier
    high, low = tokens

    def step(pair):
        return hop(pair[0], "z", 1), hop(pair[1], "z", -1)

    high_1 = step((high, high))
    low_1 = step((low, low))
    crossed = lax.ppermute(w, ("core", "x_hi"), [(1, 2), (2, 1)])
    route = [
        ((l * 2 + c) * 2 + a, ((1 - l) * 2 + a) * 2 + c)
        for l in range(2)
        for c in range(2)
        for a in range(2)
    ]
    other = lax.ppermute(w, ("x_lo", "core", "x_hi"), route)
    pair = jnp.stack([jnp.where(core == x_hi, w, crossed), other])

    high_1, pair, tables = tie((high_1, pair, tables))
    high_2 = step(high_1)
    w_ahead, w_behind = hop(pair, "y", 1), hop(pair, "y", -1)
    pair_swapped = swap(pair, "core")

    high_2, low_1 = tie((high_2, low_1))
    high_3 = step(high_2)
    low_2 = step(low_1)

    low_2, w_ahead, w_behind = tie((low_2, w_ahead, w_behind))
    low_3 = step(low_2)
    route = [(i * 2 + c, (i + 1 - 2 * c) % 4 * 2 + c) for i in range(4) for c in range(2)]
    opposite = lax.ppermute(jnp.where(core == 0, w_ahead, w_behind), ("y", "core"), route)
    ahead_swapped, behind_swapped = swap(w_ahead, "core"), swap(w_behind, "core")

    high_3, low_2 = tie((high_3, low_2))
    high_4 = hop(high_3[0], "z", 1)
    blocks = [pair, w_ahead, opposite, w_behind]
    blocks += [pair_swapped, ahead_swapped, swap(opposite, "core"), behind_swapped]
    weights = collect(where, blocks)

    low_4 = hop(low_3[1], "z", -1)

    shards = [
        [high, *high_1, *high_2, *high_3, high_4],
        [low, *low_1, *low_2, *low_3, low_4],
    ]
    return shards, weights, tables


def collect_kernel(where_ref, *refs):
    blocks, out_ref, sems = refs[:8], refs[8], refs[9]
    y_rel, x_rel, keep = where_ref[0], where_ref[1], where_ref[2]
    n = blocks[0].shape[-1]
    for half in range(2):
        columns = pl.ds(pl.multiple_of((half ^ keep) * n, n), n)
        for x in range(2):
            for k in range(4):
                place = (x ^ x_rel) * 4 + ((y_rel - k) & 3)
                pltpu.make_async_copy(
                    blocks[half * 4 + k].at[x],
                    out_ref.at[place, :, columns],
                    sems.at[(half * 2 + x) * 4 + k],
                ).start()
    for half in range(2):
        for x in range(2):
            for k in range(4):
                pltpu.make_async_copy(
                    blocks[half * 4 + k].at[x],
                    out_ref.at[0, :, pl.ds(0, n)],
                    sems.at[(half * 2 + x) * 4 + k],
                ).wait()


def collect(where, blocks):
    _, k, n = blocks[0].shape
    anywhere = pl.BlockSpec(memory_space=pl.ANY)
    return pl.pallas_call(
        collect_kernel,
        out_shape=jax.ShapeDtypeStruct((8, k, 2 * n), jnp.bfloat16),
        in_specs=[pl.BlockSpec(memory_space=pltpu.SMEM)] + [anywhere] * 8,
        out_specs=pl.BlockSpec(memory_space=pltpu.VMEM),
        scratch_shapes=[pltpu.SemaphoreType.DMA((16,))],
        compiler_params=pltpu.CompilerParams(vmem_limit_bytes=VMEM_BYTES),
        cost_estimate=pl.CostEstimate(flops=0, bytes_accessed=4 * 8 * k * n, transcendentals=0),
    )(where, *blocks)


def product_kernel(half, z_ref, weights_ref, *refs):
    tokens, out_ref = refs[:-1], refs[-1]
    z = z_ref[0]
    width = weights_ref.shape[-1] // 2
    lhs = jnp.concatenate([t[...] for t in tokens], axis=0)
    rhs = jnp.concatenate(
        [weights_ref[(z + d + 8) & 7, :, pl.ds(half * width, width)] for d in DISTANCES], axis=0
    )
    total = lax.dot_general(
        lhs, rhs, (((0,), (0,)), ((), ())), preferred_element_type=jnp.float32
    )
    out_ref[...] = total.astype(out_ref.dtype)


def product(z, shards, weights, half, dtype):
    depth, rows = shards[0].shape
    width = weights.shape[-1] // 2
    vmem = pl.BlockSpec(memory_space=pltpu.VMEM)
    return pl.pallas_call(
        functools.partial(product_kernel, half),
        out_shape=jax.ShapeDtypeStruct((rows, width), dtype),
        in_specs=[pl.BlockSpec(memory_space=pltpu.SMEM)] + [vmem] * 9,
        out_specs=vmem,
        compiler_params=pltpu.CompilerParams(vmem_limit_bytes=VMEM_BYTES),
        cost_estimate=pl.CostEstimate(
            flops=2 * 8 * depth * rows * width,
            bytes_accessed=2 * 8 * depth * (rows + width),
            transcendentals=0,
        ),
    )(z, weights, *shards)


def finish_kernel(keep_ref, sent_ref, cos_ref, sin_ref, q_ref, kv_ref):
    cos, sin = cos_ref[...], sin_ref[...]
    for j in range(4):
        columns = pl.ds(j * HEAD, HEAD)
        block = keep_ref[:, columns] + sent_ref[:, columns].astype(jnp.float32)
        if j < 3:
            block = block * cos + pltpu.roll(block, HEAD // 2, 1) * sin
        block = block.astype(jnp.bfloat16)
        if j < 2:
            q_ref[:, columns] = block
        else:
            kv_ref[:, pl.ds((j - 2) * HEAD, HEAD)] = block


def finish(keep, sent, cos, sin):
    rows = keep.shape[0]
    vmem = pl.BlockSpec(memory_space=pltpu.VMEM)
    return pl.pallas_call(
        finish_kernel,
        out_shape=[jax.ShapeDtypeStruct((rows, 2 * HEAD), jnp.bfloat16)] * 2,
        in_specs=[vmem] * 4,
        out_specs=[vmem] * 2,
        compiler_params=pltpu.CompilerParams(vmem_limit_bytes=VMEM_BYTES),
        cost_estimate=pl.CostEstimate(
            flops=rows * 2048, bytes_accessed=rows * 6000, transcendentals=0
        ),
    )(keep, sent, cos, sin)


def attend_kernel(plan, n_keys, has_state, last, joins, first_ref, q_ref, *refs):
    keys, refs = refs[:n_keys], refs[n_keys:]
    state, refs = (refs[:3], refs[3:]) if has_state else (None, refs)
    if joins:
        below_ref, refs = refs[0], refs[1:]
        refs[0][pl.ds(len(plan) * TILE, below_ref.shape[0]), :] = below_ref[...]
    outside = jnp.where(first_ref[0] == 0, jnp.float32(MASKED), jnp.float32(0))
    row = lax.broadcasted_iota(jnp.int32, (2 * TILE, TILE), 0) % TILE
    column = lax.broadcasted_iota(jnp.int32, (2 * TILE, TILE), 1)
    later = column > row
    factor = SCALE * LOG2E
    for i, tiles in enumerate(plan):
        rows = pl.ds(i * TILE, TILE)
        both = pl.ds(i * 2 * TILE, 2 * TILE)
        q = jnp.concatenate([q_ref[rows, :HEAD], q_ref[rows, HEAD:]], axis=0)
        scores = []
        for source, tile, before, masked in tiles:
            s = lax.dot_general(
                q,
                keys[source][pl.ds(tile * TILE, TILE), :HEAD],
                (((1,), (1,)), ((), ())),
                preferred_element_type=jnp.float32,
            )
            if before:
                s = s + outside
            if masked:
                s = jnp.where(later, s, MASKED) if before else jnp.where(later, MASKED, s)
            scores.append(s)
        highest = jnp.max(functools.reduce(jnp.maximum, scores), axis=-1, keepdims=True)
        highest = jnp.broadcast_to(highest, (2 * TILE, HEAD))
        if has_state:
            highest = jnp.maximum(highest, state[0][both, :])
        shift = highest * factor
        wide = jnp.concatenate([shift] * (TILE // HEAD), axis=1)
        total, summed = None, None
        for s, (source, tile, _, _) in zip(scores, tiles):
            p = jnp.exp2(s * factor - wide)
            total = p if total is None else total + p
            part = jnp.dot(
                p.astype(jnp.bfloat16),
                keys[source][pl.ds(tile * TILE, TILE), HEAD:],
                preferred_element_type=jnp.float32,
            )
            summed = part if summed is None else summed + part
        total = jnp.broadcast_to(jnp.sum(total, axis=-1, keepdims=True), (2 * TILE, HEAD))
        if has_state:
            shrink = jnp.exp2(state[0][both, :] * factor - shift)
            total = total + state[1][both, :] * shrink
            summed = summed + state[2][both, :] * shrink
        if last:
            out = (summed / total).astype(jnp.bfloat16)
            refs[0][rows, :HEAD] = out[:TILE]
            refs[0][rows, HEAD:] = out[TILE:]
        else:
            refs[0][both, :] = highest
            refs[1][both, :] = total
            refs[2][both, :] = summed


def attend(first, queries, keys, plan, state, last, below=None):
    rows = queries.shape[0]
    vmem = pl.BlockSpec(memory_space=pltpu.VMEM)
    operands = [first, queries, *keys] + ([] if state is None else list(state))
    if below is not None:
        operands.append(below)
    if last:
        joined = rows + (0 if below is None else below.shape[0])
        shapes = [jax.ShapeDtypeStruct((joined, 2 * HEAD), jnp.bfloat16)]
    else:
        shapes = [jax.ShapeDtypeStruct((2 * rows, HEAD), jnp.float32)] * 3
    pairs = sum(len(tiles) for tiles in plan) * 2 * TILE * TILE
    result = pl.pallas_call(
        functools.partial(
            attend_kernel, plan, len(keys), state is not None, last, below is not None
        ),
        out_shape=shapes,
        in_specs=[pl.BlockSpec(memory_space=pltpu.SMEM)] + [vmem] * (len(operands) - 1),
        out_specs=[vmem] * len(shapes),
        compiler_params=pltpu.CompilerParams(vmem_limit_bytes=VMEM_BYTES),
        cost_estimate=pl.CostEstimate(
            flops=4 * pairs * HEAD, bytes_accessed=rows * 4096, transcendentals=pairs
        ),
    )(*operands)
    return result[0] if last else result


def rotary_tables(positions):
    half = HEAD // 2
    inverse = jnp.power(ROPE_BASE, -2.0 * jnp.arange(half, dtype=jnp.float32) / HEAD)
    angles = positions.astype(jnp.float32)[:, None] * inverse[None, :]
    cos, sin = jnp.cos(angles), jnp.sin(angles)
    return jnp.concatenate([cos, cos], axis=1), jnp.concatenate([-sin, sin], axis=1)


def on_device(tokens, w_qkv):
    row_count = tokens.shape[0]
    rows = row_count // 2
    x_lo, y, core, z, x_hi = (lax.axis_index(a) for a in AXES)
    ctx = (x_lo * 4 + y) * 2 + core
    positions = ctx * row_count + jnp.arange(row_count, dtype=jnp.int32)
    cos, sin = rotary_tables(positions)

    z_place = z.astype(jnp.int32)[None]
    where = jnp.stack([y, x_lo, jnp.where(core == x_hi, 0, 1)]).astype(jnp.int32)

    spans = (slice(rows, row_count), slice(0, rows))
    shards, weights, (cos, sin) = gather(
        [tokens[span].T for span in spans], w_qkv, where, (cos, sin)
    )

    tie = lax.optimization_barrier
    send_high = product(z_place, shards[0], weights, 1, jnp.bfloat16)
    sent_high = swap(send_high, "x_hi")
    send_high, z_place = tie((send_high, z_place))
    send_low = product(z_place, shards[1], weights, 1, jnp.bfloat16)
    sent_low = swap(send_low, "x_hi")
    send_low, z_place = tie((send_low, z_place))
    keep_high, keep_low = (product(z_place, s, weights, 0, jnp.float32) for s in shards)
    sent_high, keep_high, keep_low = tie((sent_high, keep_high, keep_low))
    q_high, own_high = finish(keep_high, sent_high, cos[rows:], sin[rows:])
    before_high = lax.ppermute(own_high, CTX, [(c, c + 1) for c in range(15)])
    q_low, own_low = finish(keep_low, sent_low, cos[:rows], sin[:rows])
    before_low = lax.ppermute(own_low, CTX, [(c, c + 1) for c in range(15)])

    first = ctx.astype(jnp.int32)[None]
    high = attend(
        first,
        q_high,
        [before_high, own_high],
        (
            ((0, 0, True, True), (0, 1, True, False), (1, 0, False, True)),
            ((0, 1, True, True), (1, 0, False, False), (1, 1, False, True)),
        ),
        None,
        False,
    )
    high = attend(
        first, q_high, [own_low], (((0, 0, False, False), (0, 1, False, False)),) * 2, high, True
    )
    low = attend(
        first,
        q_low,
        [before_high, own_low],
        (
            ((0, 0, True, False), (0, 1, True, False), (1, 0, False, True)),
            ((0, 0, True, False), (0, 1, True, False), (1, 0, False, False), (1, 1, False, True)),
        ),
        None,
        False,
    )
    return attend(
        first,
        q_low,
        [before_low],
        (((0, 0, True, True), (0, 1, True, False)), ((0, 1, True, True),)),
        low,
        True,
        high,
    )


def solution(mesh):
    fine = Mesh(mesh.devices.reshape(SIZES), AXES)
    placed = P(CTX, HEADS)
    return jax.shard_map(
        on_device, mesh=fine, in_specs=(placed, placed), out_specs=placed, check_vma=False
    )
```

```python
import functools

import jax
import jax.numpy as jnp
from jax import lax
from jax.experimental import pallas as pl
from jax.experimental.pallas import tpu as pltpu
from jax.sharding import Mesh
from jax.sharding import PartitionSpec as P

HEAD = 128
Q_PER_KV = 2
WINDOW = 1024
ROPE_BASE = 10000.0
SCALE = 168.0 ** (-0.5)
LOG2E = 1.4426950408889634
MASKED = -1e30

AXES = ("x_lo", "y", "core", "z", "x_hi")
SIZES = (2, 4, 2, 8, 2)
CTX = ("x_lo", "y", "core")
HEADS = ("z", "x_hi")

TILE = 256
DISTANCES = (0, -1, 1, -2, 2, -3, 3, 4)
VMEM_BYTES = 12 * 1024 * 1024


def hop(block, axis, distance):
    n = lax.axis_size(axis)
    return lax.ppermute(block, axis, [(i, (i + distance) % n) for i in range(n)])


def swap(block, axis):
    return lax.ppermute(block, axis, [(0, 1), (1, 0)])


def after(value, *others):
    return lax.optimization_barrier((value, *others))[0]


def gather(tokens, w, where, tables):
    core, x_hi = lax.axis_index("core"), lax.axis_index("x_hi")
    tie = lax.optimization_barrier
    high, low = tokens

    def step(pair):
        return hop(pair[0], "z", 1), hop(pair[1], "z", -1)

    high_1 = step((high, high))
    low_1 = step((low, low))
    crossed = lax.ppermute(w, ("core", "x_hi"), [(1, 2), (2, 1)])
    route = [
        ((l * 2 + c) * 2 + a, ((1 - l) * 2 + a) * 2 + c)
        for l in range(2)
        for c in range(2)
        for a in range(2)
    ]
    other = lax.ppermute(w, ("x_lo", "core", "x_hi"), route)
    pair = jnp.stack([jnp.where(core == x_hi, w, crossed), other])

    high_1, pair, tables = tie((high_1, pair, tables))
    high_2 = step(high_1)
    w_ahead, w_behind = hop(pair, "y", 1), hop(pair, "y", -1)
    pair_swapped = swap(pair, "core")

    high_2, low_1 = tie((high_2, low_1))
    high_3 = step(high_2)
    low_2 = step(low_1)

    low_2, w_ahead, w_behind = tie((low_2, w_ahead, w_behind))
    low_3 = step(low_2)
    route = [(i * 2 + c, (i + 1 - 2 * c) % 4 * 2 + c) for i in range(4) for c in range(2)]
    opposite = lax.ppermute(jnp.where(core == 0, w_ahead, w_behind), ("y", "core"), route)
    ahead_swapped, behind_swapped = swap(w_ahead, "core"), swap(w_behind, "core")

    high_3, low_2 = tie((high_3, low_2))
    high_4 = hop(high_3[0], "z", 1)
    blocks = [pair, w_ahead, opposite, w_behind]
    blocks += [pair_swapped, ahead_swapped, swap(opposite, "core"), behind_swapped]
    weights = collect(where, blocks)

    low_4 = hop(low_3[1], "z", -1)

    shards = [
        [high, *high_1, *high_2, *high_3, high_4],
        [low, *low_1, *low_2, *low_3, low_4],
    ]
    return shards, weights, tables


def collect_kernel(where_ref, *refs):
    blocks, out_ref, sems = refs[:8], refs[8], refs[9]
    y_rel, x_rel, keep = where_ref[0], where_ref[1], where_ref[2]
    n = blocks[0].shape[-1]
    for half in range(2):
        columns = pl.ds(pl.multiple_of((half ^ keep) * n, n), n)
        for x in range(2):
            for k in range(4):
                place = (x ^ x_rel) * 4 + ((y_rel - k) & 3)
                pltpu.make_async_copy(
                    blocks[half * 4 + k].at[x],
                    out_ref.at[place, :, columns],
                    sems.at[(half * 2 + x) * 4 + k],
                ).start()
    for half in range(2):
        for x in range(2):
            for k in range(4):
                pltpu.make_async_copy(
                    blocks[half * 4 + k].at[x],
                    out_ref.at[0, :, pl.ds(0, n)],
                    sems.at[(half * 2 + x) * 4 + k],
                ).wait()


def collect(where, blocks):
    _, k, n = blocks[0].shape
    anywhere = pl.BlockSpec(memory_space=pl.ANY)
    return pl.pallas_call(
        collect_kernel,
        out_shape=jax.ShapeDtypeStruct((8, k, 2 * n), jnp.bfloat16),
        in_specs=[pl.BlockSpec(memory_space=pltpu.SMEM)] + [anywhere] * 8,
        out_specs=pl.BlockSpec(memory_space=pltpu.VMEM),
        scratch_shapes=[pltpu.SemaphoreType.DMA((16,))],
        compiler_params=pltpu.CompilerParams(vmem_limit_bytes=VMEM_BYTES),
        cost_estimate=pl.CostEstimate(flops=0, bytes_accessed=4 * 8 * k * n, transcendentals=0),
    )(where, *blocks)


def product_kernel(half, z_ref, weights_ref, *refs):
    tokens, outs = refs[:8], refs[8:]
    z = z_ref[0]
    width = weights_ref.shape[-1] // 2
    lhs = jnp.concatenate([t[...] for t in tokens], axis=0)
    rhs = jnp.concatenate(
        [weights_ref[(z + d + 8) & 7, :, pl.ds(half * width, width)] for d in DISTANCES], axis=0
    )
    total = lax.dot_general(
        lhs, rhs, (((0,), (0,)), ((), ())), preferred_element_type=jnp.float32
    )
    part = width // len(outs)
    for i, out_ref in enumerate(outs):
        out_ref[...] = total[:, i * part : (i + 1) * part].astype(out_ref.dtype)


def product(z, shards, weights, half, dtype, parts=1):
    depth, rows = shards[0].shape
    width = weights.shape[-1] // 2
    vmem = pl.BlockSpec(memory_space=pltpu.VMEM)
    return pl.pallas_call(
        functools.partial(product_kernel, half),
        out_shape=[jax.ShapeDtypeStruct((rows, width // parts), dtype)] * parts,
        in_specs=[pl.BlockSpec(memory_space=pltpu.SMEM)] + [vmem] * 9,
        out_specs=[vmem] * parts,
        compiler_params=pltpu.CompilerParams(vmem_limit_bytes=VMEM_BYTES),
        cost_estimate=pl.CostEstimate(
            flops=2 * 8 * depth * rows * width,
            bytes_accessed=2 * 8 * depth * (rows + width),
            transcendentals=0,
        ),
    )(z, weights, *shards)


def finish_kernel(keep_ref, sent_ref, cos_ref, sin_ref, q_ref, kv_ref):
    cos, sin = cos_ref[...], sin_ref[...]
    for j in range(4):
        columns = pl.ds(j * HEAD, HEAD)
        block = keep_ref[:, columns] + sent_ref[:, columns].astype(jnp.float32)
        if j < 3:
            block = block * cos + pltpu.roll(block, HEAD // 2, 1) * sin
        block = block.astype(jnp.bfloat16)
        if j < 2:
            q_ref[:, columns] = block
        else:
            kv_ref[:, pl.ds((j - 2) * HEAD, HEAD)] = block


def finish(keep, sent, cos, sin):
    rows = keep.shape[0]
    vmem = pl.BlockSpec(memory_space=pltpu.VMEM)
    return pl.pallas_call(
        finish_kernel,
        out_shape=[jax.ShapeDtypeStruct((rows, 2 * HEAD), jnp.bfloat16)] * 2,
        in_specs=[vmem] * 4,
        out_specs=[vmem] * 2,
        compiler_params=pltpu.CompilerParams(vmem_limit_bytes=VMEM_BYTES),
        cost_estimate=pl.CostEstimate(
            flops=rows * 2048, bytes_accessed=rows * 6000, transcendentals=0
        ),
    )(keep, sent, cos, sin)


def finish_pair_kernel(start, turns, keep_ref, sent_ref, cos_ref, sin_ref, out_ref):
    for j, turn in enumerate(turns):
        columns = pl.ds(j * HEAD, HEAD)
        block = keep_ref[:, pl.ds((start + j) * HEAD, HEAD)]
        block = block + sent_ref[:, columns].astype(jnp.float32)
        if turn:
            block = block * cos_ref[...] + pltpu.roll(block, HEAD // 2, 1) * sin_ref[...]
        out_ref[:, columns] = block.astype(jnp.bfloat16)


def finish_pair(keep, sent, cos, sin, start, turns):
    rows = keep.shape[0]
    vmem = pl.BlockSpec(memory_space=pltpu.VMEM)
    return pl.pallas_call(
        functools.partial(finish_pair_kernel, start, turns),
        out_shape=jax.ShapeDtypeStruct((rows, 2 * HEAD), jnp.bfloat16),
        in_specs=[vmem] * 4,
        out_specs=vmem,
        compiler_params=pltpu.CompilerParams(vmem_limit_bytes=VMEM_BYTES),
        cost_estimate=pl.CostEstimate(
            flops=rows * 1024, bytes_accessed=rows * 3000, transcendentals=0
        ),
    )(keep, sent, cos, sin)


def attend_kernel(plan, n_keys, has_state, last, joins, first_ref, q_ref, *refs):
    keys, refs = refs[:n_keys], refs[n_keys:]
    state, refs = (refs[:3], refs[3:]) if has_state else (None, refs)
    if joins:
        below_ref, refs = refs[0], refs[1:]
        refs[0][pl.ds(len(plan) * TILE, below_ref.shape[0]), :] = below_ref[...]
    outside = jnp.where(first_ref[0] == 0, jnp.float32(MASKED), jnp.float32(0))
    row = lax.broadcasted_iota(jnp.int32, (2 * TILE, TILE), 0) % TILE
    column = lax.broadcasted_iota(jnp.int32, (2 * TILE, TILE), 1)
    later = column > row
    factor = SCALE * LOG2E
    for i, tiles in enumerate(plan):
        rows = pl.ds(i * TILE, TILE)
        both = pl.ds(i * 2 * TILE, 2 * TILE)
        q = jnp.concatenate([q_ref[rows, :HEAD], q_ref[rows, HEAD:]], axis=0)
        scores = []
        for source, tile, before, masked in tiles:
            s = lax.dot_general(
                q,
                keys[source][pl.ds(tile * TILE, TILE), :HEAD],
                (((1,), (1,)), ((), ())),
                preferred_element_type=jnp.float32,
            )
            if before:
                s = s + outside
            if masked:
                s = jnp.where(later, s, MASKED) if before else jnp.where(later, MASKED, s)
            scores.append(s)
        highest = jnp.max(functools.reduce(jnp.maximum, scores), axis=-1, keepdims=True)
        highest = jnp.broadcast_to(highest, (2 * TILE, HEAD))
        if has_state:
            highest = jnp.maximum(highest, state[0][both, :])
        shift = highest * factor
        wide = jnp.concatenate([shift] * (TILE // HEAD), axis=1)
        total, summed = None, None
        for s, (source, tile, _, _) in zip(scores, tiles):
            p = jnp.exp2(s * factor - wide)
            total = p if total is None else total + p
            part = jnp.dot(
                p.astype(jnp.bfloat16),
                keys[source][pl.ds(tile * TILE, TILE), HEAD:],
                preferred_element_type=jnp.float32,
            )
            summed = part if summed is None else summed + part
        total = jnp.broadcast_to(jnp.sum(total, axis=-1, keepdims=True), (2 * TILE, HEAD))
        if has_state:
            shrink = jnp.exp2(state[0][both, :] * factor - shift)
            total = total + state[1][both, :] * shrink
            summed = summed + state[2][both, :] * shrink
        if last:
            out = (summed / total).astype(jnp.bfloat16)
            refs[0][rows, :HEAD] = out[:TILE]
            refs[0][rows, HEAD:] = out[TILE:]
        else:
            refs[0][both, :] = highest
            refs[1][both, :] = total
            refs[2][both, :] = summed


def attend(first, queries, keys, plan, state, last, below=None):
    rows = queries.shape[0]
    vmem = pl.BlockSpec(memory_space=pltpu.VMEM)
    operands = [first, queries, *keys] + ([] if state is None else list(state))
    if below is not None:
        operands.append(below)
    if last:
        joined = rows + (0 if below is None else below.shape[0])
        shapes = [jax.ShapeDtypeStruct((joined, 2 * HEAD), jnp.bfloat16)]
    else:
        shapes = [jax.ShapeDtypeStruct((2 * rows, HEAD), jnp.float32)] * 3
    pairs = sum(len(tiles) for tiles in plan) * 2 * TILE * TILE
    result = pl.pallas_call(
        functools.partial(
            attend_kernel, plan, len(keys), state is not None, last, below is not None
        ),
        out_shape=shapes,
        in_specs=[pl.BlockSpec(memory_space=pltpu.SMEM)] + [vmem] * (len(operands) - 1),
        out_specs=[vmem] * len(shapes),
        compiler_params=pltpu.CompilerParams(vmem_limit_bytes=VMEM_BYTES),
        cost_estimate=pl.CostEstimate(
            flops=4 * pairs * HEAD, bytes_accessed=rows * 4096, transcendentals=pairs
        ),
    )(*operands)
    return result[0] if last else result


def rotary_tables(positions):
    half = HEAD // 2
    inverse = jnp.power(ROPE_BASE, -2.0 * jnp.arange(half, dtype=jnp.float32) / HEAD)
    angles = positions.astype(jnp.float32)[:, None] * inverse[None, :]
    cos, sin = jnp.cos(angles), jnp.sin(angles)
    return jnp.concatenate([cos, cos], axis=1), jnp.concatenate([-sin, sin], axis=1)


def on_device(tokens, w_qkv):
    row_count = tokens.shape[0]
    rows = row_count // 2
    x_lo, y, core, z, x_hi = (lax.axis_index(a) for a in AXES)
    ctx = (x_lo * 4 + y) * 2 + core
    positions = ctx * row_count + jnp.arange(row_count, dtype=jnp.int32)
    cos, sin = rotary_tables(positions)

    z_place = z.astype(jnp.int32)[None]
    where = jnp.stack([y, x_lo, jnp.where(core == x_hi, 0, 1)]).astype(jnp.int32)

    spans = (slice(rows, row_count), slice(0, rows))
    shards, weights, (cos, sin) = gather(
        [tokens[span].T for span in spans], w_qkv, where, (cos, sin)
    )

    tie = lax.optimization_barrier
    (send_high,) = product(z_place, shards[0], weights, 1, jnp.bfloat16)
    sent_high = swap(send_high, "x_hi")
    send_high, z_place = tie((send_high, z_place))
    send_q, send_kv = product(z_place, shards[1], weights, 1, jnp.bfloat16, 2)
    sent_kv = swap(send_kv, "x_hi")
    send_kv, z_place = tie((send_kv, z_place))
    keep_high, keep_low = (product(z_place, s, weights, 0, jnp.float32)[0] for s in shards)
    send_q, keep_high = tie((send_q, keep_high))
    sent_q = swap(send_q, "x_hi")
    sent_high, keep_high, keep_low = tie((sent_high, keep_high, keep_low))
    q_high, own_high = finish(keep_high, sent_high, cos[rows:], sin[rows:])
    before_high = lax.ppermute(own_high, CTX, [(c, c + 1) for c in range(15)])
    own_low = finish_pair(keep_low, sent_kv, cos[:rows], sin[:rows], 2, (True, False))
    q_low = finish_pair(keep_low, sent_q, cos[:rows], sin[:rows], 0, (True, True))
    before_low = lax.ppermute(own_low, CTX, [(c, c + 1) for c in range(15)])

    first = ctx.astype(jnp.int32)[None]
    high = attend(
        first,
        q_high,
        [before_high, own_high],
        (
            ((0, 0, True, True), (0, 1, True, False), (1, 0, False, True)),
            ((0, 1, True, True), (1, 0, False, False), (1, 1, False, True)),
        ),
        None,
        False,
    )
    high = attend(
        first, q_high, [own_low], (((0, 0, False, False), (0, 1, False, False)),) * 2, high, True
    )
    low = attend(
        first,
        q_low,
        [before_high, own_low],
        (
            ((0, 0, True, False), (0, 1, True, False), (1, 0, False, True)),
            ((0, 0, True, False), (0, 1, True, False), (1, 0, False, False), (1, 1, False, True)),
        ),
        None,
        False,
    )
    return attend(
        first,
        q_low,
        [before_low],
        (((0, 0, True, True), (0, 1, True, False)), ((0, 1, True, True),)),
        low,
        True,
        high,
    )


def solution(mesh):
    fine = Mesh(mesh.devices.reshape(SIZES), AXES)
    placed = P(CTX, HEADS)
    return jax.shard_map(
        on_device, mesh=fine, in_specs=(placed, placed), out_specs=placed, check_vma=False
    )
```
